128 devices in a mesh: ta: 8 (over y, x_hi), col: 16 (over z, x_lo, core).
Axes of the slice: x: 4 (x_hi: 2, x_lo: 2; x = x_hi * 2 + x_lo), y: 4, z: 4, core: 2. Of those that a mesh axis runs over, the one named last changes fastest.
Arguments:
- voltages: bfloat16 [262144, 4096], P('ta', 'col'), may hold values from -6 to 6
- taps: float32 [16, 1024], replicated, may hold values from -1.5 to 1.5
- window_channels: int32 [16], replicated, may hold values from 0 to 1023
Outputs:
- visibilities: bfloat16 [16, 2, 4096, 4096], P('col', None, 'ta')
The draws below stay inside these ranges and needn't reach their ends.
Inputs may be any that keep to these rules, and one draw needn't show every extreme that they name: `window_channels`: window channels may repeat.
All inputs are finite; a program needn't handle non-finite values.
Results may differ from the reference program's by a relative error of at most 0.0056.
Values may be sent and summed in bfloat16 or wider, within the bound.
No kernel may reach another device: no remote copies, remote signals or barrier semaphores. Data moves between devices by JAX's collectives and lax.ppermute only.
A program may use at most 256 MiB of HBM per device.

```python
import math
import jax
import jax.numpy as jnp
from jax import lax

NCHAN = 1024
TAPS = 16
SIGNALS = 4096
WIN = 16
FT = 256
SAMPLES = 262144


def set_ends(values, key, low, largest):
    longest = values.shape.index(max(values.shape))
    spots = []
    for shift in (0, 1):
        where = [jax.random.randint(jax.random.fold_in(key, axis), (), 0, length) for axis, length in enumerate(values.shape)]
        where[longest] = (where[longest] + shift) % values.shape[longest]
        spots.append(tuple(where))
    return values.at[spots[0]].set(low).at[spots[1]].set(largest)


def block_levels(rng, extent, pieces, least, largest):
    def one(dim, blocks):
        steps = jax.random.uniform(jax.random.fold_in(jax.random.fold_in(rng, 6), dim), (blocks,), jnp.float32, least / len(pieces), largest / len(pieces))
        return jnp.repeat(jnp.exp(steps), extent[dim] // blocks).reshape((-1,) + (1,) * (len(extent) - dim - 1))

    loudness = one(*pieces[0])
    for cut in pieces[1:]:
        loudness = loudness * one(*cut)
    return loudness


def scatter_about(key, shape, width, bound, cuts=(), kind=jnp.bfloat16):
    array = jax.random.normal(key, shape, jnp.float32) * width
    if len(cuts) > 0:
        array = block_levels(key, shape, cuts, -0.22, 0.18) * array
    return jnp.clip(array, min=-bound, max=bound).astype(kind)


def setup_inputs(seed: int = 0) -> dict:
    key_of = jax.random.split(jax.random.key(seed), 4)
    return {
        "voltages": scatter_about(key_of[0], (SAMPLES, SIGNALS), 1.0, 6.0, ((0, 8), (1, 16))),
        "taps": scatter_about(key_of[1], (TAPS, NCHAN), 0.25, 1.5, (), jnp.float32),
        "window_channels": set_ends(jax.random.randint(key_of[2], (WIN,), 0, NCHAN), jax.random.fold_in(key_of[2], 1), 0, NCHAN - 1).astype(jnp.int32),
    }


def make_table(window_channels):
    positions = jnp.arange(NCHAN, dtype=jnp.int32)
    products = window_channels[:, None] * positions[None, :] % NCHAN
    angles = products.astype(jnp.float32) * (2.0 * math.pi / NCHAN)
    scale = 1.0 / math.sqrt(NCHAN)
    return jnp.concatenate([jnp.cos(angles) * scale, -jnp.sin(angles) * scale], 0)

def reference(voltages, taps, window_channels):
    table = make_table(window_channels)
    block = SIGNALS // 16

    def one_block(index):
        piece = lax.dynamic_slice_in_dim(voltages, (index * block).astype(jnp.int32), block, 1)
        frames = piece.astype(jnp.float32).reshape(FT, NCHAN, block)
        padded = jnp.concatenate([jnp.zeros((TAPS - 1, NCHAN, block), jnp.float32), frames], 0)
        filtered = jnp.zeros((FT, NCHAN, block), jnp.float32)
        for k in range(TAPS):
            filtered = filtered + taps[k][None, :, None] * padded[TAPS - 1 - k:TAPS - 1 - k + FT]
        spec = lax.dot_general(table, filtered, (((1,), (1,)), ((), ())), precision=lax.Precision.HIGHEST)
        return spec.astype(jnp.bfloat16)
    blocks = lax.map(one_block, jnp.arange(16, dtype=jnp.int32))
    spectra = jnp.transpose(blocks, (1, 2, 0, 3)).reshape(2 * WIN, FT, SIGNALS)

    def one_channel(index):
        real_part = lax.dynamic_index_in_dim(spectra, index, 0, keepdims=False)
        imag_part = lax.dynamic_index_in_dim(spectra, index + WIN, 0, keepdims=False)
        right = jnp.concatenate([real_part, imag_part], 0)
        rotated = jnp.concatenate([imag_part, -real_part], 0)
        dims = (((0,), (0,)), ((), ()))
        real_vis = lax.dot_general(right, right, dims, preferred_element_type=jnp.float32)
        imag_vis = lax.dot_general(rotated, right, dims, preferred_element_type=jnp.float32)
        return (jnp.stack([real_vis, imag_vis], 0) * (1.0 / FT)).astype(jnp.bfloat16)
    return lax.map(one_channel, jnp.arange(WIN, dtype=jnp.int32))
```

```python
import functools
import math

import jax
import jax.numpy as jnp
from jax import lax
from jax.experimental import pallas as pl
from jax.experimental.pallas import tpu as pltpu
from jax.sharding import PartitionSpec as P

NCHAN = 1024
TAPS = 16
NWIN = 16
ROWS = 2 * NWIN
STEP = 4
PAD = STEP - 1
HALF = 16
WIDTH = 256
LANES = 128
VMEM = 56 * 1024 * 1024

RISING = [(1 + STEP * j, min(STEP, 15 - STEP * j), TAPS - STEP * (j + 1), TAPS) for j in range(4)]
FALLING = [(STEP * j, STEP, 0, TAPS - STEP * j) for j in range(4)]


def build_coefficients(channels_ref, taps_ref, coef_ref):
    where = lax.broadcasted_iota(jnp.int32, (NWIN, NCHAN), 1)
    angles = ((channels_ref[...] * where) & (NCHAN - 1)).astype(jnp.float32) * (2.0 * math.pi / NCHAN)
    scale = 1.0 / math.sqrt(NCHAN)
    table = jnp.concatenate([jnp.cos(angles) * scale, -jnp.sin(angles) * scale], 0)
    for k in range(TAPS):
        whole = taps_ref[k : k + 1, :] * table
        high = whole.astype(jnp.bfloat16)
        low = (whole - high.astype(jnp.float32)).astype(jnp.bfloat16)
        coef_ref[2 * ROWS * k : 2 * ROWS * k + ROWS, :] = high
        coef_ref[2 * ROWS * k + ROWS : 2 * ROWS * (k + 1), :] = low


def accumulate(groups, base, volt_ref, coef_ref, frames, acc, sems):
    first = groups[0][0]

    def copy(f):
        rows = pl.ds(pl.multiple_of(f * NCHAN, NCHAN), NCHAN)
        return pltpu.make_async_copy(volt_ref.at[rows, :], frames.at[f - first], sems.at[f - first])

    for start, count, k0, k1 in groups:

        def one(i, carry, start=start, k0=k0, k1=k1):
            f = start + i
            copy(f).wait()
            got = jnp.dot(
                coef_ref[2 * ROWS * k0 : 2 * ROWS * k1, :],
                frames[f - first],
                preferred_element_type=jnp.float32,
            )
            for k in range(k0, k1):
                part = got[2 * ROWS * (k - k0) : 2 * ROWS * (k - k0 + 1)]
                rows = pl.ds(pl.multiple_of((PAD + f + k - base) * ROWS, ROWS), ROWS)
                both = part[:ROWS] + part[ROWS:]
                for lane in range(2):
                    acc[lane, rows, :] += both[:, lane * LANES : (lane + 1) * LANES]
            return carry

        lax.fori_loop(0, count, one, 0)


def start_copies(groups, volt_ref, frames, sems):
    first = groups[0][0]
    last = groups[-1][0] + groups[-1][1]

    def one(f, carry):
        rows = pl.ds(pl.multiple_of(f * NCHAN, NCHAN), NCHAN)
        pltpu.make_async_copy(volt_ref.at[rows, :], frames.at[f - first], sems.at[f - first]).start()
        return carry

    lax.fori_loop(first, last, one, 0)


def emit(acc, first, out_ref):
    for row in range(ROWS):
        part, window = divmod(row, NWIN)
        for lane in range(2):
            picked = acc[lane, pl.ds(first * ROWS + row, HALF, stride=ROWS), :]
            place = (window, slice(part * HALF, (part + 1) * HALF), slice(lane * LANES, (lane + 1) * LANES))
            out_ref[place] = picked.astype(jnp.bfloat16)


def shifted(groups, by):
    return [(start + by, count, k0, k1) for start, count, k0, k1 in groups]


def late_kernel(volt_ref, channels_ref, taps_ref, out_ref, coef_ref, frames, acc, sems):
    groups = RISING + shifted(FALLING, HALF)
    start_copies(groups, volt_ref, frames, sems)
    build_coefficients(channels_ref, taps_ref, coef_ref)
    acc[...] = jnp.zeros_like(acc)
    accumulate(groups, HALF, volt_ref, coef_ref, frames, acc, sems)
    emit(acc, PAD, out_ref)


def tail_kernel(volt_ref, coef_ref, out_ref, frames, acc, sems):
    groups = shifted(RISING, HALF)
    start_copies(groups, volt_ref, frames, sems)
    acc[...] = jnp.zeros_like(acc)
    accumulate(groups, 2 * HALF, volt_ref, coef_ref, frames, acc, sems)
    out_ref[...] = acc[:, PAD * ROWS : (PAD + TAPS - 1) * ROWS, :]


def early_kernel(volt_ref, coef_ref, out_ref, frames, acc, sems):
    groups = FALLING
    start_copies(groups, volt_ref, frames, sems)
    acc[...] = jnp.zeros_like(acc)
    accumulate(groups, 0, volt_ref, coef_ref, frames, acc, sems)
    out_ref[...] = acc[:, PAD * ROWS : (PAD + HALF) * ROWS, :]


def join_kernel(own_ref, incoming_ref, out_ref, acc):
    acc[...] = own_ref[...]
    acc[:, : (TAPS - 1) * ROWS, :] += incoming_ref[...]
    emit(acc, 0, out_ref)


def in_vmem():
    return pl.BlockSpec(memory_space=pltpu.VMEM)


def filter_scratch(count):
    return [
        pltpu.VMEM((count, NCHAN, WIDTH), jnp.bfloat16),
        pltpu.VMEM((2, (HALF + 2 * PAD) * ROWS, LANES), jnp.float32),
        pltpu.SemaphoreType.DMA((count,)),
    ]


def params():
    return pltpu.CompilerParams(vmem_limit_bytes=VMEM)


def half_shape():
    return jax.ShapeDtypeStruct((NWIN, 2 * HALF, WIDTH), jnp.bfloat16)


def correlate_kernel(count, place_ref, *refs):
    left_refs, right_refs = refs[:count], refs[count : 2 * count]
    out_ref, left = refs[2 * count :]
    rows = left.shape[0] // 2
    depth = left.shape[1]

    @pl.when(pl.program_id(0) == 0)
    def _():
        for j in range(rows // WIDTH):
            real_first = jnp.concatenate([ref[j] for ref in left_refs], 0)
            turned = []
            for ref in left_refs:
                turned += [ref[j, HALF:], -ref[j, :HALF]]
            imag_first = jnp.concatenate(turned, 0)
            left[j * WIDTH : (j + 1) * WIDTH, :] = real_first.T
            left[rows + j * WIDTH : rows + (j + 1) * WIDTH, :] = imag_first.T

    for j in range(right_refs[0].shape[0]):
        right = jnp.concatenate([ref[j] for ref in right_refs], 0)
        got = jnp.dot(left[...], right, preferred_element_type=jnp.float32) * (2.0 / depth)
        got = got.astype(jnp.bfloat16)
        out_ref[0, 0, :, j * WIDTH : (j + 1) * WIDTH] = got[:rows]
        out_ref[0, 1, :, j * WIDTH : (j + 1) * WIDTH] = got[rows:]


def correlate(place, parts, ncol, rows):
    count = len(parts)
    cols = 2
    block = (cols, 2 * HALF, WIDTH)
    left = pl.BlockSpec((rows // WIDTH, 2 * HALF, WIDTH), lambda i, place: (place[0], 0, 0))
    right = pl.BlockSpec(block, lambda i, place: (i, 0, 0))
    return pl.pallas_call(
        functools.partial(correlate_kernel, count),
        grid_spec=pltpu.PrefetchScalarGridSpec(
            num_scalar_prefetch=1,
            grid=(ncol // cols,),
            in_specs=[left] * count + [right] * count,
            out_specs=pl.BlockSpec((1, 2, rows, cols * WIDTH), lambda i, place: (0, 0, 0, i)),
            scratch_shapes=[pltpu.VMEM((2 * rows, 2 * HALF * count), jnp.bfloat16)],
        ),
        out_shape=jax.ShapeDtypeStruct((1, 2, rows, ncol * WIDTH), jnp.bfloat16),
        compiler_params=params(),
        name="correlate",
    )(place, *parts, *parts)


def moved(array, dy, dx):
    pairs = [(t, (t // 2 + dy) % 4 * 2 + (t + dx) % 2) for t in range(8)]
    return lax.ppermute(array, "ta", pairs)


def gathered(array, way):
    parts = []
    for part in (array, moved(array, 0, 1)):
        up, down = moved(part, 1, 0), moved(part, -1, 0)
        parts += [part, up, down, moved(up if way > 0 else down, way, 0)]
    return parts


def shards(voltages, taps, window_channels):
    channels = window_channels.reshape(NWIN, 1)
    anywhere = pl.BlockSpec(memory_space=pl.ANY)
    late, coef = pl.pallas_call(
        late_kernel,
        out_shape=(half_shape(), jax.ShapeDtypeStruct((2 * ROWS * TAPS, NCHAN), jnp.bfloat16)),
        in_specs=[anywhere, in_vmem(), in_vmem()],
        out_specs=(in_vmem(), in_vmem()),
        scratch_shapes=filter_scratch(31),
        compiler_params=params(),
        name="late_frames",
    )(voltages, channels, taps)
    tail = pl.pallas_call(
        tail_kernel,
        out_shape=jax.ShapeDtypeStruct((2, (TAPS - 1) * ROWS, LANES), jnp.float32),
        in_specs=[anywhere, in_vmem()],
        out_specs=in_vmem(),
        scratch_shapes=filter_scratch(15),
        compiler_params=params(),
        name="tail_frames",
    )(voltages, coef)
    incoming = lax.ppermute(tail, "ta", [(t, t + 1) for t in range(7)])
    own = pl.pallas_call(
        early_kernel,
        out_shape=jax.ShapeDtypeStruct((2, HALF * ROWS, LANES), jnp.float32),
        in_specs=[anywhere, in_vmem()],
        out_specs=in_vmem(),
        scratch_shapes=filter_scratch(16),
        compiler_params=params(),
        name="early_frames",
    )(voltages, coef)
    early = pl.pallas_call(
        join_kernel,
        out_shape=half_shape(),
        in_specs=[in_vmem(), in_vmem()],
        out_specs=in_vmem(),
        scratch_shapes=[pltpu.VMEM((2, HALF * ROWS, LANES), jnp.float32)],
        compiler_params=params(),
        name="join",
    )(own, incoming)
    late = lax.all_to_all(late, "col", 0, 0, tiled=True)
    early = lax.all_to_all(early, "col", 0, 0, tiled=True)
    parts = gathered(late, 1) + gathered(early, -1)
    place = lax.axis_index("ta").astype(jnp.int32).reshape(1)
    return correlate(place, parts, 16, 512)


def solution(mesh):
    placed = (P("ta", "col"), P(), P())
    return jax.shard_map(
        shards, mesh=mesh, in_specs=placed, out_specs=P("col", None, "ta", None), check_vma=False
    )
```

```python
import functools
import math

import jax
import jax.numpy as jnp
from jax import lax
from jax.experimental import pallas as pl
from jax.experimental.pallas import tpu as pltpu
from jax.sharding import PartitionSpec as P

NCHAN = 1024
TAPS = 16
NWIN = 16
ROWS = 2 * NWIN
STEP = 4
FULL = 16
PAD = STEP
HALF = 16
WIDTH = 256
LANES = 128
VMEM = 40 * 1024 * 1024

def build_coefficients(channels_ref, taps_ref, coef_ref):
    where = lax.broadcasted_iota(jnp.int32, (NWIN, NCHAN), 1)
    window = lax.broadcasted_iota(jnp.int32, (NWIN, NCHAN), 0)
    channels = jnp.zeros((NWIN, NCHAN), jnp.int32)
    for w in range(NWIN):
        channels = jnp.where(window == w, channels_ref[w], channels)
    angles = ((channels * where) & (NCHAN - 1)).astype(jnp.float32) * (2.0 * math.pi / NCHAN)
    scale = 1.0 / math.sqrt(NCHAN)
    table = jnp.concatenate([jnp.cos(angles) * scale, -jnp.sin(angles) * scale], 0)
    for k in range(TAPS):
        whole = taps_ref[k : k + 1, :] * table
        high = whole.astype(jnp.bfloat16)
        low = (whole - high.astype(jnp.float32)).astype(jnp.bfloat16)
        coef_ref[2 * ROWS * k : 2 * ROWS * k + ROWS, :] = high
        coef_ref[2 * ROWS * k + ROWS : 2 * ROWS * (k + 1), :] = low


def frame_copy(f, volt_ref, frames, sems):
    rows = pl.ds(pl.multiple_of(f * NCHAN, NCHAN), NCHAN)
    return pltpu.make_async_copy(volt_ref.at[rows, :], frames.at[f], sems.at[f])


def start_copies(volt_ref, frames, sems):
    def one(f, carry):
        frame_copy(f, volt_ref, frames, sems).start()
        return carry

    lax.fori_loop(0, frames.shape[0], one, 0)


def wait_frames(f, volt_ref, frames, sems):
    for u in range(STEP):
        frame_copy(f + u, volt_ref, frames, sems).wait()


def product(f, k0, taps, base, coef_ref, frames, acc):
    top = pl.multiple_of(k0 * 2 * ROWS, 2 * ROWS)
    got = jnp.dot(
        coef_ref[pl.ds(top, 2 * ROWS * taps), :],
        jnp.concatenate([frames[f + u] for u in range(STEP)], 1),
        preferred_element_type=jnp.float32,
    )
    for o in range(taps + STEP - 1):
        rows = pl.ds(pl.multiple_of((PAD + f + k0 + o - base) * ROWS, ROWS), ROWS)
        for lane in range(2):
            total = acc[lane, rows, :]
            for u in range(STEP):
                if 0 <= o - u < taps:
                    top = 2 * ROWS * (o - u)
                    cols = slice(u * WIDTH + lane * LANES, u * WIDTH + (lane + 1) * LANES)
                    total += got[top : top + ROWS, cols] + got[top + ROWS : top + 2 * ROWS, cols]
            acc[lane, rows, :] = total


def products(first, last, taps, start_of, end_of, base, volt_ref, coef_ref, frames, acc, sems):
    def group(j, carry):
        f = j * STEP
        wait_frames(f, volt_ref, frames, sems)

        def unit(q, carry):
            product(f, q * taps, taps, base, coef_ref, frames, acc)
            return carry

        return lax.fori_loop(start_of(j), end_of(j), unit, carry)

    lax.fori_loop(first, last, group, 0)


def emit(acc, first, out_ref):
    for row in range(ROWS):
        part, window = divmod(row, NWIN)
        for lane in range(2):
            picked = acc[lane, pl.ds(first * ROWS + row, HALF, stride=ROWS), :]
            place = (slice(part * HALF, (part + 1) * HALF), slice(lane * LANES, (lane + 1) * LANES))
            out_ref[(window,) + place] = picked.astype(jnp.bfloat16)


def late_kernel(volt_ref, channels_ref, taps_ref, out_ref, tail_ref, coef_ref, frames, acc, sems):
    args = (HALF, volt_ref, coef_ref, frames, acc, sems)
    groups = HALF // STEP
    start_copies(volt_ref, frames, sems)
    build_coefficients(channels_ref, taps_ref, coef_ref)
    acc[...] = jnp.zeros_like(acc)
    products(0, groups, STEP, lambda j: groups - 1 - j, lambda j: groups, *args)
    products(groups, 2 * groups, FULL, lambda j: 0, lambda j: TAPS // FULL, *args)
    emit(acc, PAD, out_ref)
    tail_ref[...] = acc[:, (PAD + HALF) * ROWS : (PAD + HALF + TAPS - 1) * ROWS, :]


def early_kernel(volt_ref, coef_ref, out_ref, frames, acc, sems):
    groups = HALF // STEP
    start_copies(volt_ref, frames, sems)
    acc[...] = jnp.zeros_like(acc)
    products(0, groups, STEP, lambda j: 0, lambda j: groups - j, 0, volt_ref, coef_ref, frames, acc, sems)
    out_ref[...] = acc[:, PAD * ROWS : (PAD + HALF) * ROWS, :]


def join_kernel(own_ref, incoming_ref, out_ref, acc):
    acc[...] = own_ref[...]
    acc[:, : (TAPS - 1) * ROWS, :] += incoming_ref[...]
    emit(acc, 0, out_ref)


def in_vmem():
    return pl.BlockSpec(memory_space=pltpu.VMEM)


def filter_scratch(count, blocks):
    return [
        pltpu.VMEM((count, NCHAN, WIDTH), jnp.bfloat16),
        pltpu.VMEM((2, blocks * ROWS, LANES), jnp.float32),
        pltpu.SemaphoreType.DMA((count,)),
    ]


def params():
    return pltpu.CompilerParams(vmem_limit_bytes=VMEM)


def half_shape():
    return jax.ShapeDtypeStruct((NWIN, 2 * HALF, WIDTH), jnp.bfloat16)


def correlate_kernel(count, place_ref, *refs):
    left_refs, right_refs = refs[:count], refs[count : 2 * count]
    out_ref, left = refs[2 * count :]
    rows = left.shape[0] // 2
    depth = left.shape[1]

    @pl.when(pl.program_id(0) == 0)
    def _():
        for j in range(rows // WIDTH):
            real_first = jnp.concatenate([ref[j] for ref in left_refs], 0)
            turned = []
            for ref in left_refs:
                turned += [ref[j, HALF:], -ref[j, :HALF]]
            imag_first = jnp.concatenate(turned, 0)
            left[j * WIDTH : (j + 1) * WIDTH, :] = real_first.T
            left[rows + j * WIDTH : rows + (j + 1) * WIDTH, :] = imag_first.T

    for j in range(right_refs[0].shape[0]):
        right = jnp.concatenate([ref[j] for ref in right_refs], 0)
        got = jnp.dot(left[...], right, preferred_element_type=jnp.float32) * (2.0 / depth)
        got = got.astype(jnp.bfloat16)
        out_ref[0, 0, :, j * WIDTH : (j + 1) * WIDTH] = got[:rows]
        out_ref[0, 1, :, j * WIDTH : (j + 1) * WIDTH] = got[rows:]


def correlate(place, parts, ncol, rows):
    count = len(parts)
    cols = 2
    left, right = [], []
    for _, first in parts:
        offset = first // cols
        block = (cols, 2 * HALF, WIDTH)
        left.append(pl.BlockSpec(block, lambda i, place, offset=offset: (place[0] + offset, 0, 0)))
        right.append(pl.BlockSpec(block, lambda i, place, offset=offset: (i + offset, 0, 0)))
    arrays = [array for array, _ in parts]
    return pl.pallas_call(
        functools.partial(correlate_kernel, count),
        grid_spec=pltpu.PrefetchScalarGridSpec(
            num_scalar_prefetch=1,
            grid=(ncol // cols,),
            in_specs=left + right,
            out_specs=pl.BlockSpec((1, 2, rows, cols * WIDTH), lambda i, place: (0, 0, 0, i)),
            scratch_shapes=[pltpu.VMEM((2 * rows, 2 * HALF * count), jnp.bfloat16)],
        ),
        out_shape=jax.ShapeDtypeStruct((1, 2, rows, ncol * WIDTH), jnp.bfloat16),
        compiler_params=params(),
        name="correlate",
    )(place, *arrays, *arrays)


def moved(array, dy, dx):
    pairs = [(t, (t // 2 + dy) % 4 * 2 + (t + dx) % 2) for t in range(8)]
    return lax.ppermute(array, "ta", pairs)


def around(array, way):
    up, down = moved(array, 1, 0), moved(array, -1, 0)
    return [array, up, down, moved(up if way > 0 else down, way, 0)]


def shards(voltages, taps, window_channels):
    anywhere = pl.BlockSpec(memory_space=pl.ANY)
    late, tail, coef = pl.pallas_call(
        late_kernel,
        out_shape=(
            half_shape(),
            jax.ShapeDtypeStruct((2, (TAPS - 1) * ROWS, LANES), jnp.float32),
            jax.ShapeDtypeStruct((2 * ROWS * TAPS, NCHAN), jnp.bfloat16),
        ),
        in_specs=[anywhere, pl.BlockSpec(memory_space=pltpu.SMEM), in_vmem()],
        out_specs=(in_vmem(),) * 3,
        scratch_shapes=filter_scratch(2 * HALF, PAD + HALF + TAPS - 1),
        compiler_params=params(),
        name="late_frames",
    )(voltages, window_channels, taps)
    incoming = lax.ppermute(tail, "ta", [(t, t + 1) for t in range(7)])
    own = pl.pallas_call(
        early_kernel,
        out_shape=jax.ShapeDtypeStruct((2, HALF * ROWS, LANES), jnp.float32),
        in_specs=[anywhere, in_vmem()],
        out_specs=in_vmem(),
        scratch_shapes=filter_scratch(HALF, PAD + HALF + STEP),
        compiler_params=params(),
        name="early_frames",
    )(voltages, coef)
    early = pl.pallas_call(
        join_kernel,
        out_shape=half_shape(),
        in_specs=[in_vmem(), in_vmem()],
        out_specs=in_vmem(),
        scratch_shapes=[pltpu.VMEM((2, HALF * ROWS, LANES), jnp.float32)],
        compiler_params=params(),
        name="join",
    )(own, incoming)
    late = lax.all_to_all(late, "col", 0, 0, tiled=True)
    late, early = lax.optimization_barrier((late, early))
    along_y = around(late, 1)
    early = lax.all_to_all(early, "col", 0, 0, tiled=True)
    arrays = along_y + [moved(array, 0, 1) for array in along_y]
    arrays += around(early, -1) + around(moved(early, 0, 1), -1)
    parts = [(array, 0) for array in arrays]
    place = lax.axis_index("ta").astype(jnp.int32).reshape(1)
    return correlate(place, parts, 16, 512)


def solution(mesh):
    placed = (P("ta", "col"), P(), P())
    return jax.shard_map(
        shards, mesh=mesh, in_specs=placed, out_specs=P("col", None, "ta", None), check_vma=False
    )
```

```python
import functools
import math

import jax
import jax.numpy as jnp
from jax import lax
from jax.experimental import pallas as pl
from jax.experimental.pallas import tpu as pltpu
from jax.sharding import PartitionSpec as P

NCHAN = 1024
TAPS = 16
NWIN = 16
ROWS = 2 * NWIN
STEP = 4
LOW = 2.0**28
SMALL = jnp.float8_e5m2
HALF = 16
WIDTH = 256
LANES = 128
VMEM = 40 * 1024 * 1024

def build_coefficients(channels_ref, taps_ref, high_ref, low_ref):
    where = lax.broadcasted_iota(jnp.int32, (NWIN, NCHAN), 1)
    window = lax.broadcasted_iota(jnp.int32, (NWIN, NCHAN), 0)
    channels = jnp.zeros((NWIN, NCHAN), jnp.int32)
    for w in range(NWIN):
        channels = jnp.where(window == w, channels_ref[w], channels)
    angles = ((channels * where) & (NCHAN - 1)).astype(jnp.float32) * (2.0 * math.pi / NCHAN)
    scale = 1.0 / math.sqrt(NCHAN)
    table = jnp.concatenate([jnp.cos(angles) * scale, -jnp.sin(angles) * scale], 0)
    for k in range(TAPS):
        whole = taps_ref[k : k + 1, :] * table
        high = whole.astype(jnp.bfloat16)
        rows = slice(ROWS * k, ROWS * (k + 1))
        high_ref[rows, :] = high
        low_ref[rows, :] = ((whole - high.astype(jnp.float32)) * LOW).astype(SMALL)


def frame_copy(first, f, volt_ref, frames, sems):
    rows = pl.ds(pl.multiple_of((first + f) * NCHAN, NCHAN), NCHAN)
    return pltpu.make_async_copy(volt_ref.at[rows, :], frames.at[f], sems.at[f])


def start_copies(first, volt_ref, frames, sems):
    def one(f, carry):
        frame_copy(first, f, volt_ref, frames, sems).start()
        return carry

    lax.fori_loop(0, HALF, one, 0)


def products(first, volt_ref, high_ref, low_ref, frames, acc, sems):
    def four_frames(j, carry):
        for u in range(STEP):
            frame_copy(first, j * STEP + u, volt_ref, frames, sems).wait()
        four = jnp.concatenate([frames[j * STEP + u] for u in range(STEP)], 1)
        got = jnp.dot(high_ref[...], four, preferred_element_type=jnp.float32)
        got += jnp.dot(low_ref[...], four.astype(SMALL), preferred_element_type=jnp.float32) * (1.0 / LOW)
        for o in range(TAPS + STEP - 1):
            rows = pl.ds(pl.multiple_of((j * STEP + o) * ROWS, ROWS), ROWS)
            for lane in range(2):
                total = acc[lane, rows, :]
                for u in range(STEP):
                    if 0 <= o - u < TAPS:
                        cols = slice(u * WIDTH + lane * LANES, u * WIDTH + (lane + 1) * LANES)
                        total += got[ROWS * (o - u) : ROWS * (o - u + 1), cols]
                acc[lane, rows, :] = total
        return carry

    lax.fori_loop(0, HALF // STEP, four_frames, 0)


def emit(acc, first, out_ref):
    for row in range(ROWS):
        part, window = divmod(row, NWIN)
        for lane in range(2):
            picked = acc[lane, pl.ds(first * ROWS + row, HALF, stride=ROWS), :]
            place = (slice(part * HALF, (part + 1) * HALF), slice(lane * LANES, (lane + 1) * LANES))
            out_ref[(window,) + place] = picked.astype(jnp.bfloat16)


def late_kernel(volt_ref, channels_ref, taps_ref, part_ref, tail_ref, high_ref, low_ref, frames, acc, sems):
    start_copies(HALF, volt_ref, frames, sems)
    build_coefficients(channels_ref, taps_ref, high_ref, low_ref)
    acc[...] = jnp.zeros_like(acc)
    products(HALF, volt_ref, high_ref, low_ref, frames, acc, sems)
    part_ref[...] = acc[:, : HALF * ROWS, :]
    tail_ref[...] = acc[:, HALF * ROWS : (HALF + TAPS - 1) * ROWS, :]


def early_kernel(volt_ref, high_ref, low_ref, part_ref, own_ref, out_ref, frames, acc, sems):
    start_copies(0, volt_ref, frames, sems)
    acc[:, : HALF * ROWS, :] = jnp.zeros_like(part_ref)
    acc[:, HALF * ROWS :, :] = part_ref[...]
    products(0, volt_ref, high_ref, low_ref, frames, acc, sems)
    emit(acc, HALF, out_ref)
    own_ref[...] = acc[:, : HALF * ROWS, :]


def join_kernel(own_ref, incoming_ref, out_ref, acc):
    acc[...] = own_ref[...]
    acc[:, : (TAPS - 1) * ROWS, :] += incoming_ref[...]
    emit(acc, 0, out_ref)


def in_vmem():
    return pl.BlockSpec(memory_space=pltpu.VMEM)


def filter_scratch():
    return [
        pltpu.VMEM((HALF, NCHAN, WIDTH), jnp.bfloat16),
        pltpu.VMEM((2, 2 * HALF * ROWS, LANES), jnp.float32),
        pltpu.SemaphoreType.DMA((HALF,)),
    ]


def params():
    return pltpu.CompilerParams(vmem_limit_bytes=VMEM)


def half_shape():
    return jax.ShapeDtypeStruct((NWIN, 2 * HALF, WIDTH), jnp.bfloat16)


def correlate_kernel(count, place_ref, *refs):
    left_refs, right_refs = refs[:count], refs[count : 2 * count]
    out_ref, left = refs[2 * count :]
    rows = left.shape[0] // 2
    depth = left.shape[1]

    @pl.when(pl.program_id(0) == 0)
    def _():
        for j in range(rows // WIDTH):
            real_first = jnp.concatenate([ref[j] for ref in left_refs], 0)
            turned = []
            for ref in left_refs:
                turned += [ref[j, HALF:], -ref[j, :HALF]]
            imag_first = jnp.concatenate(turned, 0)
            left[j * WIDTH : (j + 1) * WIDTH, :] = real_first.T
            left[rows + j * WIDTH : rows + (j + 1) * WIDTH, :] = imag_first.T

    for j in range(0, right_refs[0].shape[0], 2):
        right = jnp.concatenate(
            [jnp.concatenate([ref[j + u] for ref in right_refs], 0) for u in range(2)], 1
        )
        got = jnp.dot(left[...], right, preferred_element_type=jnp.float32) * (2.0 / depth)
        got = got.astype(jnp.bfloat16)
        out_ref[0, 0, :, j * WIDTH : (j + 2) * WIDTH] = got[:rows]
        out_ref[0, 1, :, j * WIDTH : (j + 2) * WIDTH] = got[rows:]


def correlate(place, arrays, ncol, rows):
    count = len(arrays)
    cols = 4
    near = rows // WIDTH
    left = [pl.BlockSpec((near, 2 * HALF, WIDTH), lambda i, place: (place[0], 0, 0))] * count
    right = [pl.BlockSpec((cols, 2 * HALF, WIDTH), lambda i, place: (i, 0, 0))] * count
    return pl.pallas_call(
        functools.partial(correlate_kernel, count),
        grid_spec=pltpu.PrefetchScalarGridSpec(
            num_scalar_prefetch=1,
            grid=(ncol // cols,),
            in_specs=left + right,
            out_specs=pl.BlockSpec((1, 2, rows, cols * WIDTH), lambda i, place: (0, 0, 0, i)),
            scratch_shapes=[pltpu.VMEM((2 * rows, 2 * HALF * count), jnp.bfloat16)],
        ),
        out_shape=jax.ShapeDtypeStruct((1, 2, rows, ncol * WIDTH), jnp.bfloat16),
        compiler_params=params(),
        name="correlate",
    )(place, *arrays, *arrays)


def moved(array, dy, dx):
    pairs = [(t, (t // 2 + dy) % 4 * 2 + (t + dx) % 2) for t in range(8)]
    return lax.ppermute(array, "ta", pairs)


def around(array, way):
    up, down = moved(array, 1, 0), moved(array, -1, 0)
    return [array, up, down, moved(up if way > 0 else down, way, 0)]


def shards(voltages, taps, window_channels):
    anywhere = pl.BlockSpec(memory_space=pl.ANY)
    half = jax.ShapeDtypeStruct((2, HALF * ROWS, LANES), jnp.float32)
    part, tail, high, low = pl.pallas_call(
        late_kernel,
        out_shape=(
            half,
            jax.ShapeDtypeStruct((2, (TAPS - 1) * ROWS, LANES), jnp.float32),
            jax.ShapeDtypeStruct((ROWS * TAPS, NCHAN), jnp.bfloat16),
            jax.ShapeDtypeStruct((ROWS * TAPS, NCHAN), SMALL),
        ),
        in_specs=[anywhere, pl.BlockSpec(memory_space=pltpu.SMEM), in_vmem()],
        out_specs=(in_vmem(),) * 4,
        scratch_shapes=filter_scratch(),
        compiler_params=params(),
        name="late_frames",
    )(voltages, window_channels, taps)
    incoming = lax.ppermute(tail, "ta", [(t, t + 1) for t in range(7)])
    own, late = pl.pallas_call(
        early_kernel,
        out_shape=(half, half_shape()),
        in_specs=[anywhere, in_vmem(), in_vmem(), in_vmem()],
        out_specs=(in_vmem(),) * 2,
        scratch_shapes=filter_scratch(),
        compiler_params=params(),
        name="early_frames",
    )(voltages, high, low, part)
    early = pl.pallas_call(
        join_kernel,
        out_shape=half_shape(),
        in_specs=[in_vmem(), in_vmem()],
        out_specs=in_vmem(),
        scratch_shapes=[pltpu.VMEM((2, HALF * ROWS, LANES), jnp.float32)],
        compiler_params=params(),
        name="join",
    )(own, incoming)
    late = lax.all_to_all(late, "col", 0, 0, tiled=True)
    late, early = lax.optimization_barrier((late, early))
    along_y = around(late, -1)
    early = lax.all_to_all(early, "col", 0, 0, tiled=True)
    arrays = along_y + [moved(array, 0, 1) for array in along_y]
    arrays += around(early, 1) + around(moved(early, 0, 1), -1)
    place = lax.axis_index("ta").astype(jnp.int32).reshape(1)
    return correlate(place, arrays, 16, 512)


def solution(mesh):
    placed = (P("ta", "col"), P(), P())
    return jax.shard_map(
        shards, mesh=mesh, in_specs=placed, out_specs=P("col", None, "ta", None), check_vma=False
    )
```

```python
import functools
import math

import jax
import jax.numpy as jnp
from jax import lax
from jax.experimental import pallas as pl
from jax.experimental.pallas import tpu as pltpu
from jax.sharding import PartitionSpec as P

NCHAN = 1024
TAPS = 16
NWIN = 16
ROWS = 2 * NWIN
STEP = 4
LOW = 2.0**28
SMALL = jnp.float8_e5m2
HALF = 16
WIDTH = 256
LANES = 128
MIB = 1024 * 1024
COLS = 4
SPAN = 2

def build_coefficients(channels_ref, taps_ref, high_ref, low_ref):
    where = lax.broadcasted_iota(jnp.int32, (NWIN, NCHAN), 1)
    window = lax.broadcasted_iota(jnp.int32, (NWIN, NCHAN), 0)
    channels = jnp.zeros((NWIN, NCHAN), jnp.int32)
    for w in range(NWIN):
        channels = jnp.where(window == w, channels_ref[w], channels)
    angles = ((channels * where) & (NCHAN - 1)).astype(jnp.float32) * (2.0 * math.pi / NCHAN)
    scale = 1.0 / math.sqrt(NCHAN)
    table = jnp.concatenate([jnp.cos(angles) * scale, -jnp.sin(angles) * scale], 0)
    for k in range(TAPS):
        whole = taps_ref[k : k + 1, :] * table
        high = whole.astype(jnp.bfloat16)
        rows = slice(ROWS * k, ROWS * (k + 1))
        high_ref[rows, :] = high
        low_ref[rows, :] = ((whole - high.astype(jnp.float32)) * LOW).astype(SMALL)


def frame_copy(first, f, volt_ref, frames, sems):
    rows = pl.ds(pl.multiple_of((first + f) * NCHAN, NCHAN), NCHAN)
    return pltpu.make_async_copy(volt_ref.at[rows, :], frames.at[f], sems.at[f])


def start_copies(first, volt_ref, frames, sems):
    def one(f, carry):
        frame_copy(first, f, volt_ref, frames, sems).start()
        return carry

    lax.fori_loop(0, HALF, one, 0)


def products(first, volt_ref, high_ref, low_ref, frames, acc, sems):
    def four_frames(j, carry):
        for u in range(STEP):
            frame_copy(first, j * STEP + u, volt_ref, frames, sems).wait()
        four = jnp.concatenate([frames[j * STEP + u] for u in range(STEP)], 1)
        got = jnp.dot(high_ref[...], four, preferred_element_type=jnp.float32)
        got += jnp.dot(low_ref[...], four.astype(SMALL), preferred_element_type=jnp.float32) * (1.0 / LOW)
        for o in range(TAPS + STEP - 1):
            rows = pl.ds(pl.multiple_of((j * STEP + o) * ROWS, ROWS), ROWS)
            for lane in range(2):
                total = acc[lane, rows, :]
                for u in range(STEP):
                    if 0 <= o - u < TAPS:
                        cols = slice(u * WIDTH + lane * LANES, u * WIDTH + (lane + 1) * LANES)
                        total += got[ROWS * (o - u) : ROWS * (o - u + 1), cols]
                acc[lane, rows, :] = total
        return carry

    lax.fori_loop(0, HALF // STEP, four_frames, 0)


def emit(acc, first, out_ref):
    for row in range(ROWS):
        part, window = divmod(row, NWIN)
        for lane in range(2):
            picked = acc[lane, pl.ds(first * ROWS + row, HALF, stride=ROWS), :]
            place = (slice(part * HALF, (part + 1) * HALF), slice(lane * LANES, (lane + 1) * LANES))
            out_ref[(window,) + place] = picked.astype(jnp.bfloat16)


def late_kernel(volt_ref, channels_ref, taps_ref, part_ref, tail_ref, high_ref, low_ref, frames, acc, sems):
    start_copies(HALF, volt_ref, frames, sems)
    build_coefficients(channels_ref, taps_ref, high_ref, low_ref)
    acc[...] = jnp.zeros_like(acc)
    products(HALF, volt_ref, high_ref, low_ref, frames, acc, sems)
    part_ref[...] = acc[:, : HALF * ROWS, :]
    tail_ref[...] = acc[:, HALF * ROWS : (HALF + TAPS - 1) * ROWS, :]


def early_kernel(volt_ref, high_ref, low_ref, part_ref, own_ref, out_ref, frames, acc, sems):
    start_copies(0, volt_ref, frames, sems)
    acc[:, : HALF * ROWS, :] = jnp.zeros_like(part_ref)
    acc[:, HALF * ROWS :, :] = part_ref[...]
    products(0, volt_ref, high_ref, low_ref, frames, acc, sems)
    emit(acc, HALF, out_ref)
    own_ref[...] = acc[:, : HALF * ROWS, :]


def join_kernel(own_ref, incoming_ref, out_ref, acc):
    acc[...] = own_ref[...]
    acc[:, : (TAPS - 1) * ROWS, :] += incoming_ref[...]
    emit(acc, 0, out_ref)


def in_vmem():
    return pl.BlockSpec(memory_space=pltpu.VMEM)


def filter_scratch():
    return [
        pltpu.VMEM((HALF, NCHAN, WIDTH), jnp.bfloat16),
        pltpu.VMEM((2, 2 * HALF * ROWS, LANES), jnp.float32),
        pltpu.SemaphoreType.DMA((HALF,)),
    ]


def params(mib):
    return pltpu.CompilerParams(vmem_limit_bytes=mib * MIB)


def half_shape():
    return jax.ShapeDtypeStruct((NWIN, 2 * HALF, WIDTH), jnp.bfloat16)


def turn_left(place, refs, left):
    rows = left.shape[0] // 2
    near = rows // WIDTH
    for j in range(near):
        blocks = [ref[place * near + j] for ref in refs]
        real_first = jnp.concatenate(blocks, 0)
        turned = []
        for block in blocks:
            turned += [block[HALF:], -block[:HALF]]
        imag_first = jnp.concatenate(turned, 0)
        left[j * WIDTH : (j + 1) * WIDTH, :] = real_first.T
        left[rows + j * WIDTH : rows + (j + 1) * WIDTH, :] = imag_first.T


def correlate_kernel(count, cols, last, place_ref, *refs):
    blocks, sums_ref, left = refs[:count], refs[count], refs[-1]
    rows = left.shape[0] // 2
    step = pl.program_id(0)

    @pl.when(step == 0)
    def _():
        turn_left(place_ref[0], blocks, left)

    for j in range(0, cols, SPAN):
        right = jnp.concatenate(
            [jnp.concatenate([ref[step * cols + j + u] for ref in blocks], 0) for u in range(SPAN)], 1
        )
        got = jnp.dot(left[...], right, preferred_element_type=jnp.float32)
        span = step * (cols // SPAN) + j // SPAN
        if not last:
            sums_ref[span] = got
            continue
        got = ((got + sums_ref[span]) * (1.0 / (NWIN * NWIN))).astype(jnp.bfloat16)
        place = slice(j * WIDTH, (j + SPAN) * WIDTH)
        out_ref = refs[count + 1]
        out_ref[0, 0, :, place] = got[:rows]
        out_ref[0, 1, :, place] = got[rows:]


def correlate(place, arrays, sums, ncol, rows):
    count = len(arrays)
    last = sums is not None
    cols = COLS if last else SPAN
    sums_shape = jax.ShapeDtypeStruct((ncol // SPAN, 2 * rows, SPAN * WIDTH), jnp.float32)
    out_shape = jax.ShapeDtypeStruct((1, 2, rows, ncol * WIDTH), jnp.bfloat16)
    out_block = pl.BlockSpec((1, 2, rows, cols * WIDTH), lambda i, place: (0, 0, 0, i))
    return pl.pallas_call(
        functools.partial(correlate_kernel, count, cols, last),
        grid_spec=pltpu.PrefetchScalarGridSpec(
            num_scalar_prefetch=1,
            grid=(ncol // cols,),
            in_specs=[in_vmem()] * (count + last),
            out_specs=out_block if last else in_vmem(),
            scratch_shapes=[pltpu.VMEM((2 * rows, 2 * HALF * count), jnp.bfloat16)],
        ),
        out_shape=out_shape if last else sums_shape,
        compiler_params=params(24),
        name="correlate_rest" if last else "correlate_some",
    )(place, *arrays, *([sums] * last))


def moved(array, dy, dx):
    pairs = [(t, (t // 2 + dy) % 4 * 2 + (t + dx) % 2) for t in range(8)]
    return lax.ppermute(array, "ta", pairs)


def around(array, way):
    up, down = moved(array, 1, 0), moved(array, -1, 0)
    return [array, up, down, moved(up if way > 0 else down, way, 0)]


def shards(voltages, taps, window_channels):
    anywhere = pl.BlockSpec(memory_space=pl.ANY)
    half = jax.ShapeDtypeStruct((2, HALF * ROWS, LANES), jnp.float32)
    part, tail, high, low = pl.pallas_call(
        late_kernel,
        out_shape=(
            half,
            jax.ShapeDtypeStruct((2, (TAPS - 1) * ROWS, LANES), jnp.float32),
            jax.ShapeDtypeStruct((ROWS * TAPS, NCHAN), jnp.bfloat16),
            jax.ShapeDtypeStruct((ROWS * TAPS, NCHAN), SMALL),
        ),
        in_specs=[anywhere, pl.BlockSpec(memory_space=pltpu.SMEM), in_vmem()],
        out_specs=(in_vmem(),) * 4,
        scratch_shapes=filter_scratch(),
        compiler_params=params(40),
        name="late_frames",
    )(voltages, window_channels, taps)
    incoming = lax.ppermute(tail, "ta", [(t, t + 1) for t in range(7)])
    own, late = pl.pallas_call(
        early_kernel,
        out_shape=(half, half_shape()),
        in_specs=[anywhere, in_vmem(), in_vmem(), in_vmem()],
        out_specs=(in_vmem(),) * 2,
        scratch_shapes=filter_scratch(),
        compiler_params=params(40),
        name="early_frames",
    )(voltages, high, low, part)
    early = pl.pallas_call(
        join_kernel,
        out_shape=half_shape(),
        in_specs=[in_vmem(), in_vmem()],
        out_specs=in_vmem(),
        scratch_shapes=[pltpu.VMEM((2, HALF * ROWS, LANES), jnp.float32)],
        compiler_params=params(40),
        name="join",
    )(own, incoming)
    late = lax.all_to_all(late, "col", 0, 0, tiled=True)
    late, early = lax.optimization_barrier((late, early))
    along_y = around(late, -1)
    early = lax.all_to_all(early, "col", 0, 0, tiled=True)
    arrays = along_y + [moved(array, 0, 1) for array in along_y]
    arrays += around(early, 1) + around(moved(early, 0, 1), -1)
    place = lax.axis_index("ta").astype(jnp.int32).reshape(1)
    sooner = [arrays[i] for i in (0, 1, 2, 4, 6, 8, 9, 10)]
    later = [arrays[i] for i in (3, 5, 7, 11, 12, 13, 14, 15)]
    sums = correlate(place, sooner, None, 16, 512)
    return correlate(place, later, sums, 16, 512)


def solution(mesh):
    placed = (P("ta", "col"), P(), P())
    return jax.shard_map(
        shards, mesh=mesh, in_specs=placed, out_specs=P("col", None, "ta", None), check_vma=False
    )
```

```python
import functools
import math

import jax
import jax.numpy as jnp
from jax import lax
from jax.experimental import pallas as pl
from jax.experimental.pallas import tpu as pltpu
from jax.sharding import PartitionSpec as P

NCHAN = 1024
TAPS = 16
NWIN = 16
ROWS = 2 * NWIN
STEP = 4
LOW = 2.0**28
SMALL = jnp.float8_e5m2
HALF = 16
WIDTH = 256
LANES = 128
MIB = 1024 * 1024
COLS = 4
SPAN = 4

def build_coefficients(channels_ref, taps_ref, high_ref, low_ref):
    where = lax.broadcasted_iota(jnp.int32, (NWIN, NCHAN), 1)
    window = lax.broadcasted_iota(jnp.int32, (NWIN, NCHAN), 0)
    channels = jnp.zeros((NWIN, NCHAN), jnp.int32)
    for w in range(NWIN):
        channels = jnp.where(window == w, channels_ref[w], channels)
    angles = ((channels * where) & (NCHAN - 1)).astype(jnp.float32) * (2.0 * math.pi / NCHAN)
    scale = 1.0 / math.sqrt(NCHAN)
    table = jnp.concatenate([jnp.cos(angles) * scale, -jnp.sin(angles) * scale], 0)
    for k in range(TAPS):
        whole = taps_ref[k : k + 1, :] * table
        high = whole.astype(jnp.bfloat16)
        rows = slice(ROWS * k, ROWS * (k + 1))
        high_ref[rows, :] = high
        low_ref[rows, :] = ((whole - high.astype(jnp.float32)) * LOW).astype(SMALL)


def frame_copy(first, f, volt_ref, frames, sems):
    rows = pl.ds(pl.multiple_of((first + f) * NCHAN, NCHAN), NCHAN)
    return pltpu.make_async_copy(volt_ref.at[rows, :], frames.at[f], sems.at[f])


def start_copies(first, volt_ref, frames, sems):
    def one(f, carry):
        frame_copy(first, f, volt_ref, frames, sems).start()
        return carry

    lax.fori_loop(0, HALF, one, 0)


def products(first, volt_ref, high_ref, low_ref, frames, acc, sems):
    def four_frames(j, carry):
        for u in range(STEP):
            frame_copy(first, j * STEP + u, volt_ref, frames, sems).wait()
        four = jnp.concatenate([frames[j * STEP + u] for u in range(STEP)], 1)
        got = jnp.dot(high_ref[...], four, preferred_element_type=jnp.float32)
        got += jnp.dot(low_ref[...], four.astype(SMALL), preferred_element_type=jnp.float32) * (1.0 / LOW)
        for o in range(TAPS + STEP - 1):
            rows = pl.ds(pl.multiple_of((j * STEP + o) * ROWS, ROWS), ROWS)
            for lane in range(2):
                total = acc[lane, rows, :]
                for u in range(STEP):
                    if 0 <= o - u < TAPS:
                        cols = slice(u * WIDTH + lane * LANES, u * WIDTH + (lane + 1) * LANES)
                        total += got[ROWS * (o - u) : ROWS * (o - u + 1), cols]
                acc[lane, rows, :] = total
        return carry

    lax.fori_loop(0, HALF // STEP, four_frames, 0)


def emit(acc, first, out_ref):
    for row in range(ROWS):
        part, window = divmod(row, NWIN)
        for lane in range(2):
            picked = acc[lane, pl.ds(first * ROWS + row, HALF, stride=ROWS), :]
            place = (slice(part * HALF, (part + 1) * HALF), slice(lane * LANES, (lane + 1) * LANES))
            out_ref[(window,) + place] = picked.astype(jnp.bfloat16)


def late_kernel(volt_ref, channels_ref, taps_ref, part_ref, tail_ref, high_ref, low_ref, frames, acc, sems):
    start_copies(HALF, volt_ref, frames, sems)
    build_coefficients(channels_ref, taps_ref, high_ref, low_ref)
    acc[...] = jnp.zeros_like(acc)
    products(HALF, volt_ref, high_ref, low_ref, frames, acc, sems)
    part_ref[...] = acc[:, : HALF * ROWS, :]
    tail_ref[...] = acc[:, HALF * ROWS : (HALF + TAPS - 1) * ROWS, :]


def early_kernel(volt_ref, high_ref, low_ref, part_ref, own_ref, out_ref, frames, acc, sems):
    start_copies(0, volt_ref, frames, sems)
    acc[:, : HALF * ROWS, :] = jnp.zeros_like(part_ref)
    acc[:, HALF * ROWS :, :] = part_ref[...]
    products(0, volt_ref, high_ref, low_ref, frames, acc, sems)
    emit(acc, HALF, out_ref)
    own_ref[...] = acc[:, : HALF * ROWS, :]


def join_kernel(own_ref, incoming_ref, out_ref, acc):
    acc[...] = own_ref[...]
    acc[:, : (TAPS - 1) * ROWS, :] += incoming_ref[...]
    emit(acc, 0, out_ref)


def in_vmem():
    return pl.BlockSpec(memory_space=pltpu.VMEM)


def filter_scratch():
    return [
        pltpu.VMEM((HALF, NCHAN, WIDTH), jnp.bfloat16),
        pltpu.VMEM((2, 2 * HALF * ROWS, LANES), jnp.float32),
        pltpu.SemaphoreType.DMA((HALF,)),
    ]


def params(mib):
    return pltpu.CompilerParams(vmem_limit_bytes=mib * MIB)


def half_shape():
    return jax.ShapeDtypeStruct((NWIN, 2 * HALF, WIDTH), jnp.bfloat16)


def turn_left(place, refs, left):
    rows = left.shape[0] // 2
    near = rows // WIDTH
    for j in range(near):
        blocks = [ref[place * near + j] for ref in refs]
        real_first = jnp.concatenate(blocks, 0)
        turned = []
        for block in blocks:
            turned += [block[HALF:], -block[:HALF]]
        imag_first = jnp.concatenate(turned, 0)
        left[j * WIDTH : (j + 1) * WIDTH, :] = real_first.T
        left[rows + j * WIDTH : rows + (j + 1) * WIDTH, :] = imag_first.T


def correlate_kernel(count, cols, last, place_ref, *refs):
    blocks, sums_ref, left = refs[:count], refs[count], refs[-1]
    rows = left.shape[0] // 2
    step = pl.program_id(0)

    @pl.when(step == 0)
    def _():
        turn_left(place_ref[0], blocks, left)

    for j in range(0, cols, SPAN):
        right = jnp.concatenate(
            [jnp.concatenate([ref[step * cols + j + u] for ref in blocks], 0) for u in range(SPAN)], 1
        )
        got = jnp.dot(left[...], right, preferred_element_type=jnp.float32)
        span = step * (cols // SPAN) + j // SPAN
        if not last:
            sums_ref[span] = got
            continue
        got = ((got + sums_ref[span]) * (1.0 / (NWIN * NWIN))).astype(jnp.bfloat16)
        place = slice(j * WIDTH, (j + SPAN) * WIDTH)
        out_ref = refs[count + 1]
        out_ref[0, 0, :, place] = got[:rows]
        out_ref[0, 1, :, place] = got[rows:]


def correlate(place, arrays, sums, ncol, rows):
    count = len(arrays)
    last = sums is not None
    cols = COLS if last else SPAN
    sums_shape = jax.ShapeDtypeStruct((ncol // SPAN, 2 * rows, SPAN * WIDTH), jnp.float32)
    out_shape = jax.ShapeDtypeStruct((1, 2, rows, ncol * WIDTH), jnp.bfloat16)
    out_block = pl.BlockSpec((1, 2, rows, cols * WIDTH), lambda i, place: (0, 0, 0, i))
    return pl.pallas_call(
        functools.partial(correlate_kernel, count, cols, last),
        grid_spec=pltpu.PrefetchScalarGridSpec(
            num_scalar_prefetch=1,
            grid=(ncol // cols,),
            in_specs=[in_vmem()] * (count + last),
            out_specs=out_block if last else in_vmem(),
            scratch_shapes=[pltpu.VMEM((2 * rows, 2 * HALF * count), jnp.bfloat16)],
        ),
        out_shape=out_shape if last else sums_shape,
        compiler_params=params(24),
        name="correlate_rest" if last else "correlate_some",
    )(place, *arrays, *([sums] * last))


def moved(array, dy, dx):
    pairs = [(t, (t // 2 + dy) % 4 * 2 + (t + dx) % 2) for t in range(8)]
    return lax.ppermute(array, "ta", pairs)


def around(array, way):
    up, down = moved(array, 1, 0), moved(array, -1, 0)
    return [array, up, down, moved(up if way > 0 else down, way, 0)]


def shards(voltages, taps, window_channels):
    anywhere = pl.BlockSpec(memory_space=pl.ANY)
    half = jax.ShapeDtypeStruct((2, HALF * ROWS, LANES), jnp.float32)
    part, tail, high, low = pl.pallas_call(
        late_kernel,
        out_shape=(
            half,
            jax.ShapeDtypeStruct((2, (TAPS - 1) * ROWS, LANES), jnp.float32),
            jax.ShapeDtypeStruct((ROWS * TAPS, NCHAN), jnp.bfloat16),
            jax.ShapeDtypeStruct((ROWS * TAPS, NCHAN), SMALL),
        ),
        in_specs=[anywhere, pl.BlockSpec(memory_space=pltpu.SMEM), in_vmem()],
        out_specs=(in_vmem(),) * 4,
        scratch_shapes=filter_scratch(),
        compiler_params=params(40),
        name="late_frames",
    )(voltages, window_channels, taps)
    incoming = lax.ppermute(tail, "ta", [(t, t + 1) for t in range(7)])
    own, late = pl.pallas_call(
        early_kernel,
        out_shape=(half, half_shape()),
        in_specs=[anywhere, in_vmem(), in_vmem(), in_vmem()],
        out_specs=(in_vmem(),) * 2,
        scratch_shapes=filter_scratch(),
        compiler_params=params(40),
        name="early_frames",
    )(voltages, high, low, part)
    early = pl.pallas_call(
        join_kernel,
        out_shape=half_shape(),
        in_specs=[in_vmem(), in_vmem()],
        out_specs=in_vmem(),
        scratch_shapes=[pltpu.VMEM((2, HALF * ROWS, LANES), jnp.float32)],
        compiler_params=params(40),
        name="join",
    )(own, incoming)
    late = lax.all_to_all(late, "col", 0, 0, tiled=True)
    late, early = lax.optimization_barrier((late, early))
    along_y = around(late, -1)
    early = lax.all_to_all(early, "col", 0, 0, tiled=True)
    arrays = along_y + [moved(array, 0, 1) for array in along_y]
    arrays += around(early, 1) + around(moved(early, 0, 1), -1)
    place = lax.axis_index("ta").astype(jnp.int32).reshape(1)
    sooner = [arrays[i] for i in (0, 1, 2, 4, 6, 8, 9, 10)]
    later = [arrays[i] for i in (3, 5, 7, 11, 12, 13, 14, 15)]
    sums = correlate(place, sooner, None, 16, 512)
    return correlate(place, later, sums, 16, 512)


def solution(mesh):
    placed = (P("ta", "col"), P(), P())
    return jax.shard_map(
        shards, mesh=mesh, in_specs=placed, out_specs=P("col", None, "ta", None), check_vma=False
    )
```

```python
import functools
import math

import jax
import jax.numpy as jnp
from jax import lax
from jax.experimental import pallas as pl
from jax.experimental.pallas import tpu as pltpu
from jax.sharding import PartitionSpec as P

NCHAN = 1024
TAPS = 16
NWIN = 16
ROWS = 2 * NWIN
STEP = 4
LOW = 2.0**28
SMALL = jnp.float8_e5m2
HALF = 16
WIDTH = 256
LANES = 128
MIB = 1024 * 1024
SPAN = 4

def build_coefficients(channels_ref, taps_ref, high_ref, low_ref):
    where = lax.broadcasted_iota(jnp.int32, (NWIN, NCHAN), 1)
    window = lax.broadcasted_iota(jnp.int32, (NWIN, NCHAN), 0)
    channels = jnp.zeros((NWIN, NCHAN), jnp.int32)
    for w in range(NWIN):
        channels = jnp.where(window == w, channels_ref[w], channels)
    angles = ((channels * where) & (NCHAN - 1)).astype(jnp.float32) * (2.0 * math.pi / NCHAN)
    scale = 1.0 / math.sqrt(NCHAN)
    table = jnp.concatenate([jnp.cos(angles) * scale, -jnp.sin(angles) * scale], 0)
    for k in range(TAPS):
        whole = taps_ref[k : k + 1, :] * table
        high = whole.astype(jnp.bfloat16)
        rows = slice(ROWS * k, ROWS * (k + 1))
        high_ref[rows, :] = high
        low_ref[rows, :] = ((whole - high.astype(jnp.float32)) * LOW).astype(SMALL)


def frame_copy(first, f, volt_ref, frames, sems):
    rows = pl.ds(pl.multiple_of((first + f) * NCHAN, NCHAN), NCHAN)
    return pltpu.make_async_copy(volt_ref.at[rows, :], frames.at[f], sems.at[f])


def start_copies(first, volt_ref, frames, sems):
    def one(f, carry):
        frame_copy(first, f, volt_ref, frames, sems).start()
        return carry

    lax.fori_loop(0, HALF, one, 0)


def products(first, volt_ref, high_ref, low_ref, frames, acc, sems):
    def four_frames(j, carry):
        for u in range(STEP):
            frame_copy(first, j * STEP + u, volt_ref, frames, sems).wait()
        four = jnp.concatenate([frames[j * STEP + u] for u in range(STEP)], 1)
        got = jnp.dot(high_ref[...], four, preferred_element_type=jnp.float32)
        got += jnp.dot(low_ref[...], four.astype(SMALL), preferred_element_type=jnp.float32) * (1.0 / LOW)
        for o in range(TAPS + STEP - 1):
            rows = pl.ds(pl.multiple_of((j * STEP + o) * ROWS, ROWS), ROWS)
            for lane in range(2):
                total = acc[lane, rows, :]
                for u in range(STEP):
                    if 0 <= o - u < TAPS:
                        cols = slice(u * WIDTH + lane * LANES, u * WIDTH + (lane + 1) * LANES)
                        total += got[ROWS * (o - u) : ROWS * (o - u + 1), cols]
                acc[lane, rows, :] = total
        return carry

    lax.fori_loop(0, HALF // STEP, four_frames, 0)


def emit(acc, first, out_ref):
    for row in range(ROWS):
        part, window = divmod(row, NWIN)
        for lane in range(2):
            picked = acc[lane, pl.ds(first * ROWS + row, HALF, stride=ROWS), :]
            place = (slice(part * HALF, (part + 1) * HALF), slice(lane * LANES, (lane + 1) * LANES))
            out_ref[(window,) + place] = picked.astype(jnp.bfloat16)


def late_kernel(volt_ref, channels_ref, taps_ref, part_ref, tail_ref, high_ref, low_ref, frames, acc, sems):
    start_copies(HALF, volt_ref, frames, sems)
    build_coefficients(channels_ref, taps_ref, high_ref, low_ref)
    acc[...] = jnp.zeros_like(acc)
    products(HALF, volt_ref, high_ref, low_ref, frames, acc, sems)
    part_ref[...] = acc[:, : HALF * ROWS, :]
    tail_ref[...] = acc[:, HALF * ROWS : (HALF + TAPS - 1) * ROWS, :]


def early_kernel(volt_ref, high_ref, low_ref, part_ref, own_ref, out_ref, frames, acc, sems):
    start_copies(0, volt_ref, frames, sems)
    acc[:, : HALF * ROWS, :] = jnp.zeros_like(part_ref)
    acc[:, HALF * ROWS :, :] = part_ref[...]
    products(0, volt_ref, high_ref, low_ref, frames, acc, sems)
    emit(acc, HALF, out_ref)
    own_ref[...] = acc[:, : HALF * ROWS, :]


def join_kernel(own_ref, incoming_ref, out_ref, acc):
    acc[...] = own_ref[...]
    acc[:, : (TAPS - 1) * ROWS, :] += incoming_ref[...]
    emit(acc, 0, out_ref)


def in_vmem():
    return pl.BlockSpec(memory_space=pltpu.VMEM)


def filter_scratch():
    return [
        pltpu.VMEM((HALF, NCHAN, WIDTH), jnp.bfloat16),
        pltpu.VMEM((2, 2 * HALF * ROWS, LANES), jnp.float32),
        pltpu.SemaphoreType.DMA((HALF,)),
    ]


def params(mib):
    return pltpu.CompilerParams(vmem_limit_bytes=mib * MIB)


def half_shape():
    return jax.ShapeDtypeStruct((NWIN, 2 * HALF, WIDTH), jnp.bfloat16)


def turn_left(place, refs, left):
    rows = left.shape[0] // 2
    near = rows // WIDTH
    for j in range(near):
        blocks = [ref[place * near + j] for ref in refs]
        real_first = jnp.concatenate(blocks, 0)
        turned = []
        for block in blocks:
            turned += [block[HALF:], -block[:HALF]]
        imag_first = jnp.concatenate(turned, 0)
        left[j * WIDTH : (j + 1) * WIDTH, :] = real_first.T
        left[rows + j * WIDTH : rows + (j + 1) * WIDTH, :] = imag_first.T


def correlate_kernel(count, last, place_ref, *refs):
    blocks, sums_ref, left = refs[:count], refs[count], refs[-1]
    rows = left.shape[0] // 2
    step = pl.program_id(0)

    @pl.when(step == 0)
    def _():
        turn_left(place_ref[0], blocks, left)

    def columns(first):
        return jnp.concatenate(
            [jnp.concatenate([ref[first + u] for ref in blocks], 0) for u in range(SPAN)], 1
        )

    if not last:
        place = pl.ds(pl.multiple_of(step * SPAN * WIDTH, SPAN * WIDTH), SPAN * WIDTH)
        sums_ref[:, place] = jnp.dot(left[...], columns(step * SPAN), preferred_element_type=jnp.float32)
        return
    out_ref = refs[count + 1]
    few = out_ref.shape[2]
    top = pl.ds(pl.multiple_of(step * few, few), few)
    bottom = pl.ds(pl.multiple_of(rows + step * few, few), few)
    both = jnp.concatenate([left[top, :], left[bottom, :]], 0)
    for j in range(0, blocks[0].shape[0], SPAN):
        place = slice(j * WIDTH, (j + SPAN) * WIDTH)
        got = jnp.dot(both, columns(j), preferred_element_type=jnp.float32)
        for part, picked in enumerate((top, bottom)):
            total = got[part * few : (part + 1) * few] + sums_ref[picked, place]
            out_ref[0, part, :, place] = (total * (1.0 / (NWIN * NWIN))).astype(jnp.bfloat16)


def correlate(place, arrays, sums, ncol, rows):
    count = len(arrays)
    last = sums is not None
    few = rows // 2
    sums_shape = jax.ShapeDtypeStruct((2 * rows, ncol * WIDTH), jnp.float32)
    out_shape = jax.ShapeDtypeStruct((1, 2, rows, ncol * WIDTH), jnp.bfloat16)
    out_block = pl.BlockSpec((1, 2, few, ncol * WIDTH), lambda i, place: (0, 0, i, 0))
    return pl.pallas_call(
        functools.partial(correlate_kernel, count, last),
        grid_spec=pltpu.PrefetchScalarGridSpec(
            num_scalar_prefetch=1,
            grid=(rows // few if last else ncol // SPAN,),
            in_specs=[in_vmem()] * (count + last),
            out_specs=out_block if last else in_vmem(),
            scratch_shapes=[pltpu.VMEM((2 * rows, 2 * HALF * count), jnp.bfloat16)],
        ),
        out_shape=out_shape if last else sums_shape,
        compiler_params=params(24),
        name="correlate_rest" if last else "correlate_some",
    )(place, *arrays, *([sums] * last))


def moved(array, dy, dx):
    pairs = [(t, (t // 2 + dy) % 4 * 2 + (t + dx) % 2) for t in range(8)]
    return lax.ppermute(array, "ta", pairs)


def around(array, way):
    up, down = moved(array, 1, 0), moved(array, -1, 0)
    return [array, up, down, moved(up if way > 0 else down, way, 0)]


def shards(voltages, taps, window_channels):
    anywhere = pl.BlockSpec(memory_space=pl.ANY)
    half = jax.ShapeDtypeStruct((2, HALF * ROWS, LANES), jnp.float32)
    part, tail, high, low = pl.pallas_call(
        late_kernel,
        out_shape=(
            half,
            jax.ShapeDtypeStruct((2, (TAPS - 1) * ROWS, LANES), jnp.float32),
            jax.ShapeDtypeStruct((ROWS * TAPS, NCHAN), jnp.bfloat16),
            jax.ShapeDtypeStruct((ROWS * TAPS, NCHAN), SMALL),
        ),
        in_specs=[anywhere, pl.BlockSpec(memory_space=pltpu.SMEM), in_vmem()],
        out_specs=(in_vmem(),) * 4,
        scratch_shapes=filter_scratch(),
        compiler_params=params(40),
        name="late_frames",
    )(voltages, window_channels, taps)
    incoming = lax.ppermute(tail, "ta", [(t, t + 1) for t in range(7)])
    own, late = pl.pallas_call(
        early_kernel,
        out_shape=(half, half_shape()),
        in_specs=[anywhere, in_vmem(), in_vmem(), in_vmem()],
        out_specs=(in_vmem(),) * 2,
        scratch_shapes=filter_scratch(),
        compiler_params=params(40),
        name="early_frames",
    )(voltages, high, low, part)
    early = pl.pallas_call(
        join_kernel,
        out_shape=half_shape(),
        in_specs=[in_vmem(), in_vmem()],
        out_specs=in_vmem(),
        scratch_shapes=[pltpu.VMEM((2, HALF * ROWS, LANES), jnp.float32)],
        compiler_params=params(40),
        name="join",
    )(own, incoming)
    late = lax.all_to_all(late, "col", 0, 0, tiled=True)
    late, early = lax.optimization_barrier((late, early))
    along_y = around(late, -1)
    early = lax.all_to_all(early, "col", 0, 0, tiled=True)
    arrays = along_y + [moved(array, 0, 1) for array in along_y]
    arrays += around(early, 1) + around(moved(early, 0, 1), -1)
    place = lax.axis_index("ta").astype(jnp.int32).reshape(1)
    sooner = [arrays[i] for i in (0, 1, 2, 4, 6, 8, 9, 10)]
    later = [arrays[i] for i in (3, 5, 7, 11, 12, 13, 14, 15)]
    sums = correlate(place, sooner, None, 16, 512)
    return correlate(place, later, sums, 16, 512)


def solution(mesh):
    placed = (P("ta", "col"), P(), P())
    return jax.shard_map(
        shards, mesh=mesh, in_specs=placed, out_specs=P("col", None, "ta", None), check_vma=False
    )
```
